512 devices in a mesh: dp: 8 (over y, core), expert: 64 (over z, x).
Axes of the slice: x: 4, y: 4, z: 16, core: 2. Of those that a mesh axis runs over, the one named last changes fastest.
Arguments:
- tokens: bfloat16 [65536, 2048], P(('dp', 'expert')), may hold values from -6 to 6
- hidden_grad: bfloat16 [65536, 1536], P(('dp', 'expert')), may hold values from -6 to 6
- gate_weight: bfloat16 [64, 1536, 2048], P('expert', 'dp'), may hold values from -0.125 to 0.125
- up_weight: bfloat16 [64, 1536, 2048], P('expert', 'dp'), may hold values from -0.125 to 0.125
- replica_offset: int32 [64], P('expert'), may hold values from 1 to 2, as said below
- block_expert: int32 [1024], P(('dp', 'expert')), may hold values from 0 to 63, as said below
- block_rows: int32 [1024], P(('dp', 'expert')), may hold values from 16 to 64, as said below
Outputs:
- input_grad: bfloat16 [65536, 2048], P(('dp', 'expert'))
- gate_grad: bfloat16 [64, 1536, 2048], P('expert', 'dp')
- up_grad: bfloat16 [64, 1536, 2048], P('expert', 'dp')
The draws below stay inside these ranges and needn't reach their ends.
Inputs may be any that keep to these rules, and one draw needn't show every extreme that they name: Host h holds a copy of expert (h - replica_offset[h]) mod 64. `block_expert`: each block's expert is either its host's own expert (the host's index on the expert axis) or the expert that the host holds a copy of. `block_rows`: every device has at least one block with all 64 rows live.
All inputs are finite; a program needn't handle non-finite values.
Results may differ from the reference program's by a relative error of at most 0.017.
Values may be sent and summed in bfloat16 or wider, within the bound.
No kernel may reach another device: no remote copies, remote signals or barrier semaphores. Data moves between devices by JAX's collectives and lax.ppermute only.
A program may use at most 64 MiB of HBM per device.

```python
import jax
import jax.numpy as jnp
from jax import lax

D = 2048
FF = 1536
BLOCK = 64
BLOCKS_DEV = 2
REACH = 2
EXPERTS = 64
TOKENS = 65536
N_DP = 8


def plan_offsets(key):
    return jax.random.randint(jax.random.fold_in(key, 11), (EXPERTS,), 1, REACH + 1).astype(jnp.int32)


def draw_replica_offset(key, part):
    return plan_offsets(key)


def draw_block_expert(key, part):
    offsets = plan_offsets(key)
    key = jax.random.fold_in(key, 5)
    blocks_all = TOKENS // BLOCK
    column_of = jnp.arange(blocks_all, dtype=jnp.int32) // BLOCKS_DEV % EXPERTS
    replica = (column_of - offsets[column_of]) % EXPERTS
    chosen = jax.random.randint(key, (blocks_all,), 0, 2)
    return jnp.where(chosen == 1, replica, column_of).astype(jnp.int32)


def draw_block_rows(key, part):
    key = jax.random.fold_in(key, 7)
    first_key, second_key = jax.random.split(key)
    blocks_all = TOKENS // BLOCK
    drawn_rows = jax.random.randint(first_key, (blocks_all,), BLOCK // 4, BLOCK + 1)
    full_slot = jax.random.randint(second_key, (blocks_all // BLOCKS_DEV,), 0, BLOCKS_DEV)
    slot_index = jnp.arange(blocks_all, dtype=jnp.int32) % BLOCKS_DEV
    return jnp.where(slot_index == jnp.repeat(full_slot, BLOCKS_DEV), BLOCK, drawn_rows).astype(jnp.int32)


def level_of(rng, shape, cuts, smallest, top_value):
    factor_of, own = 1.0, jax.random.fold_in(rng, 6)
    for dim, parts in cuts:
        heights = jnp.exp(jax.random.uniform(jax.random.fold_in(own, dim), (parts,), jnp.float32, smallest / len(cuts), top_value / len(cuts)))
        factor_of = factor_of * jnp.repeat(heights, shape[dim] // parts).reshape([-1 if axis == dim else 1 for axis in range(len(shape))])
    return factor_of


def centred(own_key, shape, scale, bound, pieces=(), held_as=jnp.bfloat16):
    array = scale * jax.random.normal(own_key, shape, jnp.float32)
    if pieces:
        array = array * level_of(own_key, shape, pieces, -0.22, 0.18)
    return jnp.clip(array, -bound, bound).astype(held_as)


def setup_inputs(seed: int = 0) -> dict:
    keys = jax.random.split(jax.random.key(seed), 8)
    tokens = centred(keys[0], (TOKENS, D), 1.0, 6.0, ((0, 512),))
    hidden_grad = centred(keys[1], (TOKENS, FF), 1.0, 6.0, ((0, 512),))
    gate_weight = centred(keys[2], (EXPERTS, FF, D), D ** -0.5, 0.125, ((0, 64), (1, 8)))
    up_weight = centred(keys[3], (EXPERTS, FF, D), D ** -0.5, 0.125, ((0, 64), (1, 8)))
    replica_offset = draw_replica_offset(jax.random.fold_in(keys[7], 71), 0)
    block_expert = draw_block_expert(jax.random.fold_in(keys[7], 71), 0)
    block_rows = draw_block_rows(jax.random.fold_in(keys[7], 71), 0)
    return {"tokens": tokens, "hidden_grad": hidden_grad, "gate_weight": gate_weight, "up_weight": up_weight, "replica_offset": replica_offset, "block_expert": block_expert, "block_rows": block_rows}


def stacked_weights(gate_weight, up_weight, index):
    shard_width = FF // N_DP
    gate_part = gate_weight[index].T.reshape(D, N_DP, 1, shard_width)
    up_part = up_weight[index].T.reshape(D, N_DP, 1, shard_width)
    return jnp.concatenate([gate_part, up_part], axis=2).reshape(D, 2 * FF)


def reference(tokens, hidden_grad, gate_weight, up_weight, replica_offset, block_expert, block_rows):
    shard_width = FF // N_DP
    rows_dev = BLOCKS_DEV * BLOCK
    row_blocks = tokens.reshape(N_DP, EXPERTS, rows_dev, D)
    cotangents = hidden_grad.reshape(N_DP, EXPERTS, rows_dev, FF)
    experts = block_expert.reshape(N_DP, EXPERTS, BLOCKS_DEV)
    lengths = block_rows.reshape(N_DP, EXPERTS, BLOCKS_DEV)

    def column(host_id):
        x_col = lax.dynamic_index_in_dim(row_blocks, host_id, 1, keepdims=False).reshape(N_DP * BLOCKS_DEV, BLOCK, D)
        dh_col = lax.dynamic_index_in_dim(cotangents, host_id, 1, keepdims=False).reshape(N_DP * BLOCKS_DEV, BLOCK, N_DP, shard_width)
        e_col = lax.dynamic_index_in_dim(experts, host_id, 1, keepdims=False).reshape(-1)
        n_col = lax.dynamic_index_in_dim(lengths, host_id, 1, keepdims=False).reshape(-1)
        source = (host_id - replica_offset[host_id]) % EXPERTS
        w_home = stacked_weights(gate_weight, up_weight, host_id)
        w_copy = stacked_weights(gate_weight, up_weight, source)

        def one_block(block_item):
            x_blk, dh_blk, e_blk, n_blk = block_item
            weights = jnp.where(e_blk == host_id, w_home, w_copy)
            projected = jnp.dot(x_blk, weights, preferred_element_type=jnp.float32).reshape(BLOCK, N_DP, 2, shard_width)
            gate_val = projected[:, :, 0]
            up_val = projected[:, :, 1]
            sig_val = jax.nn.sigmoid(gate_val)
            live_rows = (jnp.arange(BLOCK, dtype=jnp.int32) < n_blk).astype(jnp.float32)
            cotan = dh_blk.astype(jnp.float32) * live_rows[:, None, None]
            dgate = cotan * up_val * sig_val * (1.0 + gate_val * (1.0 - sig_val))
            dup = cotan * gate_val * sig_val
            dgu = jnp.stack([dgate, dup], axis=2).astype(jnp.bfloat16)
            partials = jnp.einsum('rkf,dkf->rkd', dgu.reshape(BLOCK, N_DP, 2 * shard_width).astype(jnp.float32),
                                  weights.reshape(D, N_DP, 2 * shard_width).astype(jnp.float32))
            rounded = lax.optimization_barrier(partials.astype(jnp.bfloat16))
            dx_blk = jnp.sum(rounded.astype(jnp.float32), axis=1).astype(jnp.bfloat16)
            return dgu.reshape(BLOCK, 2 * FF), dx_blk

        dgu_all, dx_all = lax.map(one_block, (x_col, dh_col, e_col, n_col))
        x_flat = x_col.reshape(-1, D)
        d_flat = dgu_all.reshape(-1, 2 * FF)
        on_home = jnp.repeat(e_col == host_id, BLOCK)[:, None]
        zeros_bf = jnp.zeros_like(d_flat)
        home_part = jnp.dot(x_flat.T, jnp.where(on_home, d_flat, zeros_bf), preferred_element_type=jnp.float32)
        copy_part = jnp.dot(x_flat.T, jnp.where(on_home, zeros_bf, d_flat), preferred_element_type=jnp.float32).astype(jnp.bfloat16)
        return dx_all.reshape(N_DP, rows_dev, D), home_part, copy_part

    dx_cols, home_all, copy_all = lax.map(column, jnp.arange(EXPERTS, dtype=jnp.int32))
    input_grad = jnp.transpose(dx_cols, (1, 0, 2, 3)).reshape(TOKENS, D)

    def combine(expert_id):
        summed = home_all[expert_id]
        for hop_index in range(1, REACH + 1):
            host_id = (expert_id + hop_index) % EXPERTS
            incoming = copy_all[host_id].astype(jnp.float32)
            summed = summed + jnp.where(replica_offset[host_id] == hop_index, incoming, jnp.zeros_like(incoming))
        reshaped = summed.reshape(D, N_DP, 2, shard_width)
        gate_out = reshaped[:, :, 0].reshape(D, FF).T.astype(jnp.bfloat16)
        up_out = reshaped[:, :, 1].reshape(D, FF).T.astype(jnp.bfloat16)
        return gate_out, up_out

    gate_grad, up_grad = lax.map(combine, jnp.arange(EXPERTS, dtype=jnp.int32))
    return input_grad, gate_grad, up_grad
```

```python
import jax
import jax.numpy as jnp
from jax import lax
from jax.sharding import PartitionSpec as P

CHIPS_X = 4
CORES = 2
FLAG_ROWS = 16


def ring_pairs(count, steps):
    return [(source, (source + steps) % count) for source in range(count)]


def ring_step(count, steps):
    return [(e, e // CHIPS_X * CHIPS_X + (e + steps) % CHIPS_X) for e in range(count)]


def onward(count, steps, total):
    return [(holder, (source + total) % count) for source, holder in ring_step(count, steps)]


def local(tokens, hidden_grad, gate_weight, up_weight, replica_offset, block_expert, block_rows):
    n_exp = lax.axis_size("expert")
    n_dp = lax.axis_size("dp")
    chips_y = n_dp // CORES
    home_id = lax.axis_index("expert")
    core = lax.axis_index("dp") % CORES
    gate_w, up_w = gate_weight[0], up_weight[0]
    shard, width = gate_w.shape
    rows = tokens.shape[0]
    nblk = block_expert.shape[0]
    block_len = rows // nblk
    ahead, behind = ring_pairs(n_exp, 1), ring_pairs(n_exp, -1)
    swap = [(d, d // CORES * CORES + (d + 1) % CORES) for d in range(n_dp)]
    same_core = [[y * CORES + c for y in range(chips_y)] for c in range(CORES)]
    zero = jnp.zeros((), jnp.bfloat16)
    barrier = lax.optimization_barrier

    def exchange_y(parts):
        return lax.all_to_all(
            parts, "dp", split_axis=0, concat_axis=0, axis_index_groups=same_core, tiled=True
        )

    offset = replica_offset[0]
    spread = jnp.broadcast_to(tokens[None], (chips_y, rows, width))
    live = (jnp.arange(block_len, dtype=jnp.int32)[None, :] < block_rows[:, None]).reshape(1, rows)
    flag = jnp.repeat((block_expert == home_id).astype(jnp.bfloat16), block_len).reshape(1, rows)
    cot = jnp.where(live, hidden_grad.T, zero).reshape(n_dp, shard, rows)
    flags = jnp.broadcast_to(flag[None], (n_dp, FLAG_ROWS, rows))
    sent = jnp.concatenate([cot, flags], axis=1)
    w_home = jnp.concatenate([gate_w, up_w], axis=0)
    gate_w, up_w, spread = barrier((gate_w, up_w, spread))
    gate_1 = lax.ppermute(gate_w, "expert", ahead)
    up_held = lax.ppermute(up_w, "expert", ring_step(n_exp, -1))
    sent, replica_offset = barrier((sent, replica_offset))
    offset_next = lax.ppermute(replica_offset, "expert", behind)[0]
    own_rows = exchange_y(spread).reshape(chips_y * rows, width)

    mixed = jnp.where(offset_next == 1, up_w, gate_1)
    mixed, up_held, own_rows = barrier((mixed, up_held, own_rows))
    mixed_1 = lax.ppermute(mixed, "expert", ahead)
    up_2 = lax.ppermute(up_held, "expert", onward(n_exp, -1, 2))
    other_rows = lax.ppermute(own_rows, "dp", swap)
    sent, other_rows = barrier((sent, other_rows))
    got = lax.all_to_all(sent, "dp", split_axis=0, concat_axis=0, tiled=True)
    got = got.reshape(chips_y, CORES, shard + FLAG_ROWS, rows)

    def cotangents(which):
        part = lax.dynamic_index_in_dim(got, which, 1, keepdims=False)
        return jnp.transpose(part, (1, 0, 2)).reshape(shard + FLAG_ROWS, chips_y * rows)

    nt = (((1,), (1,)), ((), ()))
    tn = (((0,), (0,)), ((), ()))

    def project(weights, x):
        return lax.dot_general(weights, x, nt, preferred_element_type=jnp.float32)

    halves = (own_rows, other_rows)
    cots = [cotangents(core), cotangents(1 - core)]
    home_proj = [project(w_home, x) for x in halves]
    mixed_1, up_2, home_proj, cots = barrier((mixed_1, up_2, home_proj, cots))

    w_copy = jnp.concatenate(
        [jnp.where(offset == 1, gate_1, mixed_1), jnp.where(offset == 1, mixed_1, up_2)], axis=0
    )
    home_terms, copy_terms = [], []
    for x, cot, proj in zip(halves, cots, home_proj):
        on_home = cot[shard : shard + 1] > 0.5
        both = jnp.where(on_home, proj, project(w_copy, x))
        cotan = cot[:shard].astype(jnp.float32)
        gate_val, up_val = both[:shard], both[shard:]
        sig_val = jax.nn.sigmoid(gate_val)
        dgate = (cotan * up_val * sig_val * (1.0 + gate_val * (1.0 - sig_val))).astype(jnp.bfloat16)
        dup = (cotan * gate_val * sig_val).astype(jnp.bfloat16)
        terms = jnp.concatenate([dgate, dup], axis=0)
        home_terms.append(jnp.where(on_home, terms, zero))
        copy_terms.append(jnp.where(on_home, zero, terms))

    def weight_part(terms):
        return sum(jnp.dot(t, x, preferred_element_type=jnp.float32) for t, x in zip(terms, halves))

    copy_part = weight_part(copy_terms).astype(jnp.bfloat16)
    copy_g, copy_u = copy_part[:shard], copy_part[shard:]
    first = jnp.where(offset == 1, copy_u, copy_g)
    second = jnp.where(offset == 2, copy_u, zero)
    first, second, home_terms, copy_terms, copy_g = barrier(
        (first, second, home_terms, copy_terms, copy_g)
    )

    ret_1 = lax.ppermute(first, "expert", behind)
    ret_h = lax.ppermute(second, "expert", ring_step(n_exp, 1))
    weights_all = jnp.concatenate([w_home, w_copy], axis=0)

    def rows_part(half):
        terms = jnp.concatenate([home_terms[half], copy_terms[half]], axis=0)
        return lax.dot_general(terms, weights_all, tn, preferred_element_type=jnp.float32)

    dx_oth = rows_part(1).astype(jnp.bfloat16)
    dx_in = lax.ppermute(dx_oth, "dp", swap)
    dx_own, dx_in = barrier((rows_part(0), dx_in))
    dx_pair = (dx_own + dx_in.astype(jnp.float32)).astype(jnp.bfloat16)
    ret_1, ret_h, dx_pair = barrier((ret_1, ret_h, dx_pair))
    dx_parts = exchange_y(dx_pair.reshape(chips_y, rows, width))

    sum_g = jnp.where(offset == 1, copy_g, zero).astype(jnp.float32) + jnp.where(
        offset_next == 2, ret_1, zero
    ).astype(jnp.float32)
    sum_g, ret_h, home_terms = barrier((sum_g.astype(jnp.bfloat16), ret_h, home_terms))
    ret_g = lax.ppermute(sum_g, "expert", behind)
    ret_u = lax.ppermute(ret_h, "expert", onward(n_exp, 1, -2))
    home_part = weight_part(home_terms)
    up_part = home_part[shard:] + jnp.where(offset_next == 1, ret_1, zero).astype(jnp.float32)
    gate_part = home_part[:shard]
    up_part, gate_part, dx_parts, ret_g, ret_u = barrier((up_part, gate_part, dx_parts, ret_g, ret_u))
    input_grad = jnp.sum(dx_parts.astype(jnp.float32), axis=0).astype(jnp.bfloat16)
    gate_grad = (gate_part + ret_g.astype(jnp.float32)).astype(jnp.bfloat16)
    up_grad = (up_part + ret_u.astype(jnp.float32)).astype(jnp.bfloat16)
    return input_grad, gate_grad[None], up_grad[None]


def solution(mesh):
    placed = (
        P(("dp", "expert"), None),
        P(("dp", "expert"), None),
        P("expert", "dp", None),
        P("expert", "dp", None),
        P("expert"),
        P(("dp", "expert")),
        P(("dp", "expert")),
    )
    return jax.shard_map(
        local,
        mesh=mesh,
        in_specs=placed,
        out_specs=(P(("dp", "expert"), None), P("expert", "dp", None), P("expert", "dp", None)),
        check_vma=False,
    )
```

```python
import jax
import jax.numpy as jnp
from jax import lax
from jax.sharding import PartitionSpec as P

CHIPS_X = 4
CORES = 2
FLAG_ROWS = 16


def ring_pairs(count, steps):
    return [(source, (source + steps) % count) for source in range(count)]


def ring_step(count, steps):
    return [(e, e // CHIPS_X * CHIPS_X + (e + steps) % CHIPS_X) for e in range(count)]


def onward(count, steps, total):
    return [(holder, (source + total) % count) for source, holder in ring_step(count, steps)]


def local(tokens, hidden_grad, gate_weight, up_weight, replica_offset, block_expert, block_rows):
    n_exp = lax.axis_size("expert")
    n_dp = lax.axis_size("dp")
    chips_y = n_dp // CORES
    home_id = lax.axis_index("expert")
    core = lax.axis_index("dp") % CORES
    gate_w, up_w = gate_weight[0], up_weight[0]
    shard, width = gate_w.shape
    rows = tokens.shape[0]
    nblk = block_expert.shape[0]
    block_len = rows // nblk
    ahead, behind = ring_pairs(n_exp, 1), ring_pairs(n_exp, -1)
    swap = [(d, d // CORES * CORES + (d + 1) % CORES) for d in range(n_dp)]
    same_core = [[y * CORES + c for y in range(chips_y)] for c in range(CORES)]
    zero = jnp.zeros((), jnp.bfloat16)
    barrier = lax.optimization_barrier

    def exchange_y(parts):
        return lax.all_to_all(
            parts, "dp", split_axis=0, concat_axis=0, axis_index_groups=same_core, tiled=True
        )

    offset = replica_offset[0]
    spread = jnp.broadcast_to(tokens[None], (chips_y, rows, width))
    live = (jnp.arange(block_len, dtype=jnp.int32)[None, :] < block_rows[:, None]).reshape(1, rows)
    flag = jnp.repeat((block_expert == home_id).astype(jnp.bfloat16), block_len).reshape(1, rows)
    cot = jnp.where(live, hidden_grad.T, zero).reshape(n_dp, shard, rows)
    flags = jnp.broadcast_to(flag[None], (n_dp, FLAG_ROWS, rows))
    sent = jnp.concatenate([cot, flags], axis=1)
    w_home = jnp.concatenate([gate_w, up_w], axis=0)
    gate_w, up_w, spread = barrier((gate_w, up_w, spread))
    gate_1 = lax.ppermute(gate_w, "expert", ahead)
    up_held = lax.ppermute(up_w, "expert", ring_step(n_exp, -1))
    sent, replica_offset = barrier((sent, replica_offset))
    offset_next = lax.ppermute(replica_offset, "expert", behind)[0]
    own_rows = exchange_y(spread).reshape(chips_y * rows, width)

    mixed = jnp.where(offset_next == 1, up_w, gate_1)
    mixed, up_held, own_rows = barrier((mixed, up_held, own_rows))
    up_2 = lax.ppermute(up_held, "expert", onward(n_exp, -1, 2))
    mixed_1 = lax.ppermute(mixed, "expert", ahead)
    other_rows = lax.ppermute(own_rows, "dp", swap)
    sent, other_rows = barrier((sent, other_rows))
    got = lax.all_to_all(sent, "dp", split_axis=0, concat_axis=0, tiled=True)
    got = got.reshape(chips_y, CORES, shard + FLAG_ROWS, rows)

    def cotangents(which):
        part = lax.dynamic_index_in_dim(got, which, 1, keepdims=False)
        return jnp.transpose(part, (1, 0, 2)).reshape(shard + FLAG_ROWS, chips_y * rows)

    cots = jnp.concatenate([cotangents(core), cotangents(1 - core)], axis=1)
    all_rows = jnp.concatenate([own_rows, other_rows], axis=0)
    nt = (((1,), (1,)), ((), ()))
    tn = (((0,), (0,)), ((), ()))

    def project(weights, x):
        return lax.dot_general(weights, x, nt, preferred_element_type=jnp.float32)

    home_proj = project(w_home, all_rows)
    mixed_1, home_proj, cots = barrier((mixed_1, home_proj, cots))

    on_home = cots[shard : shard + 1] > 0.5
    gate_c = jnp.where(offset == 1, gate_1, mixed_1)
    gate_val = jnp.where(on_home, home_proj[:shard], project(gate_c, all_rows))
    gate_val, up_2 = barrier((gate_val, up_2))
    up_c = jnp.where(offset == 1, mixed_1, up_2)
    up_val = jnp.where(on_home, home_proj[shard:], project(up_c, all_rows))
    cotan = cots[:shard].astype(jnp.float32)
    sig_val = jax.nn.sigmoid(gate_val)
    dgate = (cotan * up_val * sig_val * (1.0 + gate_val * (1.0 - sig_val))).astype(jnp.bfloat16)
    dup = (cotan * gate_val * sig_val).astype(jnp.bfloat16)
    terms = jnp.concatenate([dgate, dup], axis=0)
    home_terms = jnp.where(on_home, terms, zero)
    copy_terms = jnp.where(on_home, zero, terms)
    copy_part = jnp.dot(copy_terms, all_rows, preferred_element_type=jnp.float32).astype(jnp.bfloat16)
    copy_g, copy_u = copy_part[:shard], copy_part[shard:]
    first = jnp.where(offset == 1, copy_u, copy_g)
    second = jnp.where(offset == 2, copy_u, zero)
    kept = jnp.where(offset == 1, copy_g, zero)
    first, second, kept, home_terms, copy_terms = barrier(
        (first, second, kept, home_terms, copy_terms)
    )

    ret_1 = lax.ppermute(first, "expert", behind)
    ret_h = lax.ppermute(second, "expert", ring_step(n_exp, 1))
    weights_all = jnp.concatenate([w_home, gate_c, up_c], axis=0)
    both_terms = jnp.concatenate([home_terms, copy_terms], axis=0)
    half = chips_y * rows

    def rows_part(terms):
        return lax.dot_general(terms, weights_all, tn, preferred_element_type=jnp.float32)

    dx_oth = rows_part(both_terms[:, half:]).astype(jnp.bfloat16)
    dx_in = lax.ppermute(dx_oth, "dp", swap)
    dx_own, dx_in = barrier((rows_part(both_terms[:, :half]), dx_in))
    dx_pair = (dx_own + dx_in.astype(jnp.float32)).astype(jnp.bfloat16)
    dx_pair, home_terms = barrier((dx_pair, home_terms))
    dx_parts = exchange_y(dx_pair.reshape(chips_y, rows, width))

    home_part = jnp.dot(home_terms, all_rows, preferred_element_type=jnp.float32)
    ret_1, ret_h, home_part = barrier((ret_1, ret_h, home_part))
    sum_g = kept.astype(jnp.float32) + jnp.where(offset_next == 2, ret_1, zero).astype(jnp.float32)
    sum_g, ret_h, home_part = barrier((sum_g.astype(jnp.bfloat16), ret_h, home_part))
    ret_g = lax.ppermute(sum_g, "expert", behind)
    ret_u = lax.ppermute(ret_h, "expert", onward(n_exp, 1, -2))
    input_grad = jnp.sum(dx_parts.astype(jnp.float32), axis=0).astype(jnp.bfloat16)
    home_part, ret_1, input_grad, ret_g, ret_u = barrier((home_part, ret_1, input_grad, ret_g, ret_u))
    gate_grad = (home_part[:shard] + ret_g.astype(jnp.float32)).astype(jnp.bfloat16)
    up_grad = (
        home_part[shard:]
        + jnp.where(offset_next == 1, ret_1, zero).astype(jnp.float32)
        + ret_u.astype(jnp.float32)
    ).astype(jnp.bfloat16)
    return input_grad, gate_grad[None], up_grad[None]


def solution(mesh):
    placed = (
        P(("dp", "expert"), None),
        P(("dp", "expert"), None),
        P("expert", "dp", None),
        P("expert", "dp", None),
        P("expert"),
        P(("dp", "expert")),
        P(("dp", "expert")),
    )
    return jax.shard_map(
        local,
        mesh=mesh,
        in_specs=placed,
        out_specs=(P(("dp", "expert"), None), P("expert", "dp", None), P("expert", "dp", None)),
        check_vma=False,
    )
```

```python
import jax
import jax.numpy as jnp
from jax import lax
from jax.sharding import PartitionSpec as P

CHIPS_X = 4
CORES = 2
FLAG_ROWS = 16


def ring_pairs(count, steps):
    return [(source, (source + steps) % count) for source in range(count)]


def ring_step(count, steps):
    return [(e, e // CHIPS_X * CHIPS_X + (e + steps) % CHIPS_X) for e in range(count)]


def onward(count, steps, total):
    return [(holder, (source + total) % count) for source, holder in ring_step(count, steps)]


def local(tokens, hidden_grad, gate_weight, up_weight, replica_offset, block_expert, block_rows):
    n_exp = lax.axis_size("expert")
    n_dp = lax.axis_size("dp")
    chips_y = n_dp // CORES
    home_id = lax.axis_index("expert")
    place = lax.axis_index("dp")
    core = place % CORES
    gate_w, up_w = gate_weight[0], up_weight[0]
    shard, width = gate_w.shape
    rows = tokens.shape[0]
    nblk = block_expert.shape[0]
    block_len = rows // nblk
    ahead, behind = ring_pairs(n_exp, 1), ring_pairs(n_exp, -1)
    swap = [(d, d // CORES * CORES + (d + 1) % CORES) for d in range(n_dp)]
    same_core = [[y * CORES + c for y in range(chips_y)] for c in range(CORES)]
    zero = jnp.zeros((), jnp.bfloat16)
    barrier = lax.optimization_barrier

    def exchange_y(parts):
        return lax.all_to_all(
            parts, "dp", split_axis=0, concat_axis=0, axis_index_groups=same_core, tiled=True
        )

    offset = replica_offset[0]
    spread = jnp.broadcast_to(tokens[None], (chips_y, rows, width))
    live = (jnp.arange(block_len, dtype=jnp.int32)[None, :] < block_rows[:, None]).reshape(1, rows)
    flag = jnp.repeat((block_expert == home_id).astype(jnp.bfloat16), block_len).reshape(1, rows)
    cot = jnp.where(live, hidden_grad.T, zero).reshape(n_dp, shard, rows)
    flags = jnp.broadcast_to(flag[None], (n_dp, FLAG_ROWS, rows))
    sent = jnp.concatenate([cot, flags], axis=1)
    gate_1 = lax.ppermute(gate_w, "expert", ahead)
    up_held = lax.ppermute(up_w, "expert", ring_step(n_exp, -1))
    sent, replica_offset = barrier((sent, replica_offset))
    offset_next = lax.ppermute(replica_offset, "expert", behind)[0]
    own_rows = exchange_y(spread).reshape(chips_y * rows, width)

    gate_1, up_held, gate_w, up_w = barrier((gate_1, up_held, gate_w, up_w))
    mixed = jnp.where(offset_next == 1, up_w, gate_1)
    w_home = jnp.concatenate([gate_w, up_w], axis=0)
    own_rows, w_home, _ = barrier((own_rows, w_home, mixed))
    up_2 = lax.ppermute(up_held, "expert", onward(n_exp, -1, 2))
    mixed_1 = lax.ppermute(mixed, "expert", ahead)
    sent, own_rows = barrier((sent, own_rows))
    other_rows = lax.cond(
        place < n_dp, lambda v: lax.ppermute(v, "dp", swap), jnp.zeros_like, own_rows
    )
    got = lax.all_to_all(sent, "dp", split_axis=0, concat_axis=0, tiled=True)
    nt = (((1,), (1,)), ((), ()))
    tn = (((0,), (0,)), ((), ()))

    def project(weights, x):
        return lax.dot_general(weights, x, nt, preferred_element_type=jnp.float32)

    gate_c = jnp.where(offset == 1, gate_1, mixed_1)
    gate_c, mixed_1, got, other_rows, own_rows = barrier(
        (gate_c, mixed_1, got, other_rows, own_rows)
    )
    got = got.reshape(chips_y, CORES, shard + FLAG_ROWS, rows)

    def cotangents(which):
        part = lax.dynamic_index_in_dim(got, which, 1, keepdims=False)
        return jnp.transpose(part, (1, 0, 2)).reshape(shard + FLAG_ROWS, chips_y * rows)

    cots = jnp.concatenate([cotangents(core), cotangents(1 - core)], axis=1)
    all_rows = jnp.concatenate([own_rows, other_rows], axis=0)
    up_2, all_rows = barrier((up_2, all_rows))
    up_c = jnp.where(offset == 1, mixed_1, up_2)
    weights_all = jnp.concatenate([gate_w, up_w, gate_c, up_c], axis=0)
    proj = project(weights_all, all_rows)
    on_home = cots[shard : shard + 1] > 0.5
    both = jnp.where(on_home, proj[: 2 * shard], proj[2 * shard :])
    gate_val, up_val = both[:shard], both[shard:]
    cotan = cots[:shard].astype(jnp.float32)
    sig_val = jax.nn.sigmoid(gate_val)
    dgate = (cotan * up_val * sig_val * (1.0 + gate_val * (1.0 - sig_val))).astype(jnp.bfloat16)
    dup = (cotan * gate_val * sig_val).astype(jnp.bfloat16)
    terms = jnp.concatenate([dgate, dup], axis=0)
    home_terms = jnp.where(on_home, terms, zero)
    copy_terms = jnp.where(on_home, zero, terms)
    copy_part = jnp.dot(copy_terms, all_rows, preferred_element_type=jnp.float32).astype(jnp.bfloat16)
    copy_g, copy_u = copy_part[:shard], copy_part[shard:]
    first = jnp.where(offset == 1, copy_u, copy_g)
    second = jnp.where(offset == 2, copy_u, zero)
    kept = jnp.where(offset == 1, copy_g, zero)
    first, second, kept, home_terms, copy_terms = barrier(
        (first, second, kept, home_terms, copy_terms)
    )

    ret_1 = lax.ppermute(first, "expert", behind)
    ret_h = lax.ppermute(second, "expert", ring_step(n_exp, 1))
    both_terms = jnp.concatenate([home_terms, copy_terms], axis=0)
    half = chips_y * rows

    def rows_part(terms):
        return lax.dot_general(terms, weights_all, tn, preferred_element_type=jnp.float32)

    dx_oth = rows_part(both_terms[:, half:]).astype(jnp.bfloat16)
    dx_in = lax.ppermute(dx_oth, "dp", swap)
    dx_own, dx_in = barrier((rows_part(both_terms[:, :half]), dx_in))
    dx_pair = (dx_own + dx_in.astype(jnp.float32)).astype(jnp.bfloat16)
    dx_pair, home_terms = barrier((dx_pair, home_terms))
    dx_parts = exchange_y(dx_pair.reshape(chips_y, rows, width))

    home_part = jnp.dot(home_terms, all_rows, preferred_element_type=jnp.float32).astype(jnp.bfloat16)
    ret_1, ret_h, home_part = barrier((ret_1, ret_h, home_part))
    sum_g = kept.astype(jnp.float32) + jnp.where(offset_next == 2, ret_1, zero).astype(jnp.float32)
    sum_g, ret_h, home_part = barrier((sum_g.astype(jnp.bfloat16), ret_h, home_part))
    ret_g = lax.ppermute(sum_g, "expert", behind)
    ret_u = lax.ppermute(ret_h, "expert", onward(n_exp, 1, -2))
    input_grad = jnp.sum(dx_parts.astype(jnp.float32), axis=0).astype(jnp.bfloat16)
    home_part, ret_1, input_grad, ret_g, ret_u = barrier((home_part, ret_1, input_grad, ret_g, ret_u))
    gate_grad = (home_part[:shard].astype(jnp.float32) + ret_g.astype(jnp.float32)).astype(jnp.bfloat16)
    up_grad = (
        home_part[shard:].astype(jnp.float32)
        + jnp.where(offset_next == 1, ret_1, zero).astype(jnp.float32)
        + ret_u.astype(jnp.float32)
    ).astype(jnp.bfloat16)
    return input_grad, gate_grad[None], up_grad[None]


def solution(mesh):
    placed = (
        P(("dp", "expert"), None),
        P(("dp", "expert"), None),
        P("expert", "dp", None),
        P("expert", "dp", None),
        P("expert"),
        P(("dp", "expert")),
        P(("dp", "expert")),
    )
    return jax.shard_map(
        local,
        mesh=mesh,
        in_specs=placed,
        out_specs=(P(("dp", "expert"), None), P("expert", "dp", None), P("expert", "dp", None)),
        check_vma=False,
    )
```

```python
import jax
import jax.numpy as jnp
from jax import lax
from jax.sharding import PartitionSpec as P

CHIPS_X = 4
CORES = 2
FLAG_ROWS = 16


def ring_pairs(count, steps):
    return [(source, (source + steps) % count) for source in range(count)]


def ring_step(count, steps):
    return [(e, e // CHIPS_X * CHIPS_X + (e + steps) % CHIPS_X) for e in range(count)]


def onward(count, steps, total):
    return [(holder, (source + total) % count) for source, holder in ring_step(count, steps)]


def local(tokens, hidden_grad, gate_weight, up_weight, replica_offset, block_expert, block_rows):
    n_exp = lax.axis_size("expert")
    n_dp = lax.axis_size("dp")
    chips_y = n_dp // CORES
    home_id = lax.axis_index("expert")
    place = lax.axis_index("dp")
    core = place % CORES
    gate_w, up_w = gate_weight[0], up_weight[0]
    shard, width = gate_w.shape
    rows = tokens.shape[0]
    nblk = block_expert.shape[0]
    block_len = rows // nblk
    ahead, behind = ring_pairs(n_exp, 1), ring_pairs(n_exp, -1)
    swap = [(d, d // CORES * CORES + (d + 1) % CORES) for d in range(n_dp)]
    same_core = [[y * CORES + c for y in range(chips_y)] for c in range(CORES)]
    zero = jnp.zeros((), jnp.bfloat16)
    barrier = lax.optimization_barrier

    def exchange_y(parts):
        return lax.all_to_all(
            parts, "dp", split_axis=0, concat_axis=0, axis_index_groups=same_core, tiled=True
        )

    offset = replica_offset[0]
    spread = jnp.broadcast_to(tokens[None], (chips_y, rows, width))
    live = (jnp.arange(block_len, dtype=jnp.int32)[None, :] < block_rows[:, None]).reshape(1, rows)
    flag = jnp.repeat((block_expert == home_id).astype(jnp.bfloat16), block_len).reshape(1, rows)
    cot = jnp.where(live, hidden_grad.T, zero).reshape(n_dp, shard, rows)
    flags = jnp.broadcast_to(flag[None], (n_dp, FLAG_ROWS, rows))
    sent = jnp.concatenate([cot, flags], axis=1)
    gate_1 = lax.ppermute(gate_w, "expert", ahead)
    up_held = lax.ppermute(up_w, "expert", ring_step(n_exp, -1))
    sent, replica_offset = barrier((sent, replica_offset))
    offset_next = lax.ppermute(replica_offset, "expert", behind)[0]
    own_rows = exchange_y(spread).reshape(chips_y * rows, width)

    gate_1, up_held, gate_w, up_w = barrier((gate_1, up_held, gate_w, up_w))
    mixed = jnp.where(offset_next == 1, up_w, gate_1)
    w_home = jnp.concatenate([gate_w, up_w], axis=0)
    own_rows, w_home, _ = barrier((own_rows, w_home, mixed))
    up_2 = lax.ppermute(up_held, "expert", onward(n_exp, -1, 2))
    mixed_1 = lax.ppermute(mixed, "expert", ahead)
    sent, own_rows = barrier((sent, own_rows))
    other_rows = lax.cond(
        place < n_dp, lambda v: lax.ppermute(v, "dp", swap), jnp.zeros_like, own_rows
    )
    got = lax.all_to_all(sent, "dp", split_axis=0, concat_axis=0, tiled=True)
    nt = (((1,), (1,)), ((), ()))
    tn = (((0,), (0,)), ((), ()))

    def project(weights, x):
        return lax.dot_general(weights, x, nt, preferred_element_type=jnp.float32)

    gate_c = jnp.where(offset == 1, gate_1, mixed_1)
    gate_c, mixed_1, got, other_rows, own_rows = barrier(
        (gate_c, mixed_1, got, other_rows, own_rows)
    )
    got = got.reshape(chips_y, CORES, shard + FLAG_ROWS, rows)

    def cotangents(which):
        part = lax.dynamic_index_in_dim(got, which, 1, keepdims=False)
        return jnp.transpose(part, (1, 0, 2)).reshape(shard + FLAG_ROWS, chips_y * rows)

    cots = jnp.concatenate([cotangents(core), cotangents(1 - core)], axis=1)
    all_rows = jnp.concatenate([own_rows, other_rows], axis=0)
    up_2, all_rows = barrier((up_2, all_rows))
    up_c = jnp.where(offset == 1, mixed_1, up_2)
    weights_all = jnp.concatenate([gate_w, up_w, gate_c, up_c], axis=0)
    proj = project(weights_all, all_rows)
    on_home = cots[shard : shard + 1] > 0.5
    both = jnp.where(on_home, proj[: 2 * shard], proj[2 * shard :])
    gate_val, up_val = both[:shard], both[shard:]
    cotan = cots[:shard].astype(jnp.float32)
    sig_val = jax.nn.sigmoid(gate_val)
    dgate = (cotan * up_val * sig_val * (1.0 + gate_val * (1.0 - sig_val))).astype(jnp.bfloat16)
    dup = (cotan * gate_val * sig_val).astype(jnp.bfloat16)
    terms = jnp.concatenate([dgate, dup], axis=0)
    home_terms = jnp.where(on_home, terms, zero)
    copy_terms = jnp.where(on_home, zero, terms)
    copy_part = jnp.dot(copy_terms, all_rows, preferred_element_type=jnp.float32).astype(jnp.bfloat16)
    copy_g, copy_u = copy_part[:shard], copy_part[shard:]
    first = jnp.where(offset == 1, copy_u, copy_g)
    second = jnp.where(offset == 2, copy_u, zero)
    first, second, copy_g, home_terms, copy_terms = barrier(
        (first, second, copy_g, home_terms, copy_terms)
    )

    ret_1 = lax.ppermute(first, "expert", behind)
    ret_h = lax.ppermute(second, "expert", ring_step(n_exp, 1))
    both_terms = jnp.concatenate([home_terms, copy_terms], axis=0)
    half = chips_y * rows

    def rows_part(terms):
        return lax.dot_general(terms, weights_all, tn, preferred_element_type=jnp.float32)

    dx_oth = rows_part(both_terms[:, half:]).astype(jnp.bfloat16)
    dx_in = lax.ppermute(dx_oth, "dp", swap)
    dx_own, dx_in = barrier((rows_part(both_terms[:, :half]), dx_in))
    dx_pair = (dx_own + dx_in.astype(jnp.float32)).astype(jnp.bfloat16)
    dx_pair, home_terms = barrier((dx_pair, home_terms))
    dx_parts = exchange_y(dx_pair.reshape(chips_y, rows, width))

    home_part = jnp.dot(home_terms, all_rows, preferred_element_type=jnp.float32).astype(jnp.bfloat16)
    ret_1, home_part = barrier((ret_1, home_part))
    sum_g = jnp.where(offset == 1, copy_g, zero).astype(jnp.float32) + jnp.where(offset_next == 2, ret_1, zero).astype(jnp.float32)
    sum_g, home_part = barrier((sum_g.astype(jnp.bfloat16), home_part))
    ret_g = lax.ppermute(sum_g, "expert", behind)
    ret_h, _ = barrier((ret_h, sum_g))
    ret_u = lax.ppermute(ret_h, "expert", onward(n_exp, 1, -2))
    input_grad = jnp.sum(dx_parts.astype(jnp.float32), axis=0).astype(jnp.bfloat16)
    home_part, input_grad, ret_g = barrier((home_part, input_grad, ret_g))
    gate_grad = (home_part[:shard].astype(jnp.float32) + ret_g.astype(jnp.float32)).astype(jnp.bfloat16)
    gate_grad, home_part, ret_1, ret_u = barrier((gate_grad, home_part, ret_1, ret_u))
    up_grad = (
        home_part[shard:].astype(jnp.float32)
        + jnp.where(offset_next == 1, ret_1, zero).astype(jnp.float32)
        + ret_u.astype(jnp.float32)
    ).astype(jnp.bfloat16)
    return input_grad, gate_grad[None], up_grad[None]


def solution(mesh):
    placed = (
        P(("dp", "expert"), None),
        P(("dp", "expert"), None),
        P("expert", "dp", None),
        P("expert", "dp", None),
        P("expert"),
        P(("dp", "expert")),
        P(("dp", "expert")),
    )
    return jax.shard_map(
        local,
        mesh=mesh,
        in_specs=placed,
        out_specs=(P(("dp", "expert"), None), P("expert", "dp", None), P("expert", "dp", None)),
        check_vma=False,
    )
```

```python
import jax
import jax.numpy as jnp
from jax import lax
from jax.sharding import PartitionSpec as P

CHIPS_X = 4
CORES = 2
FLAG_ROWS = 16


def ring_pairs(count, steps):
    return [(source, (source + steps) % count) for source in range(count)]


def ring_step(count, steps):
    return [(e, e // CHIPS_X * CHIPS_X + (e + steps) % CHIPS_X) for e in range(count)]


def onward(count, steps, total):
    return [(holder, (source + total) % count) for source, holder in ring_step(count, steps)]


def local(tokens, hidden_grad, gate_weight, up_weight, replica_offset, block_expert, block_rows):
    n_exp = lax.axis_size("expert")
    n_dp = lax.axis_size("dp")
    chips_y = n_dp // CORES
    home_id = lax.axis_index("expert")
    place = lax.axis_index("dp")
    core = place % CORES
    gate_w, up_w = gate_weight[0], up_weight[0]
    shard, width = gate_w.shape
    rows = tokens.shape[0]
    nblk = block_expert.shape[0]
    block_len = rows // nblk
    ahead, behind = ring_pairs(n_exp, 1), ring_pairs(n_exp, -1)
    swap = [(d, d // CORES * CORES + (d + 1) % CORES) for d in range(n_dp)]
    same_core = [[y * CORES + c for y in range(chips_y)] for c in range(CORES)]
    zero = jnp.zeros((), jnp.bfloat16)
    barrier = lax.optimization_barrier

    def exchange_y(parts):
        return lax.all_to_all(
            parts, "dp", split_axis=0, concat_axis=0, axis_index_groups=same_core, tiled=True
        )

    offset = replica_offset[0]
    spread = jnp.broadcast_to(tokens[None], (chips_y, rows, width))
    live = (jnp.arange(block_len, dtype=jnp.int32)[None, :] < block_rows[:, None]).reshape(1, rows)
    flag = jnp.repeat((block_expert == home_id).astype(jnp.bfloat16), block_len).reshape(1, rows)
    cot = jnp.where(live, hidden_grad.T, zero).reshape(n_dp, shard, rows)
    flags = jnp.broadcast_to(flag[None], (n_dp, FLAG_ROWS, rows))
    sent = jnp.concatenate([cot, flags], axis=1)
    gate_1 = lax.ppermute(gate_w, "expert", ahead)
    up_held = lax.ppermute(up_w, "expert", ring_step(n_exp, -1))
    sent, replica_offset = barrier((sent, replica_offset))
    offset_next = lax.ppermute(replica_offset, "expert", behind)[0]
    own_rows = exchange_y(spread).reshape(chips_y * rows, width)

    gate_1, up_held, gate_w, up_w = barrier((gate_1, up_held, gate_w, up_w))
    mixed = jnp.where(offset_next == 1, up_w, gate_1)
    w_home = jnp.concatenate([gate_w, up_w], axis=0)
    own_rows, w_home, _ = barrier((own_rows, w_home, mixed))
    up_2 = lax.ppermute(up_held, "expert", onward(n_exp, -1, 2))
    mixed_1 = lax.ppermute(mixed, "expert", ahead)
    sent, own_rows = barrier((sent, own_rows))
    other_rows = lax.cond(
        place < n_dp, lambda v: lax.ppermute(v, "dp", swap), jnp.zeros_like, own_rows
    )
    got = lax.all_to_all(sent, "dp", split_axis=0, concat_axis=0, tiled=True)
    nt = (((1,), (1,)), ((), ()))
    tn = (((0,), (0,)), ((), ()))

    def project(weights, x):
        return lax.dot_general(weights, x, nt, preferred_element_type=jnp.float32)

    gate_c = jnp.where(offset == 1, gate_1, mixed_1)
    gate_c, mixed_1, got, other_rows, own_rows = barrier(
        (gate_c, mixed_1, got, other_rows, own_rows)
    )
    got = got.reshape(chips_y, CORES, shard + FLAG_ROWS, rows)

    def cotangents(which):
        part = lax.dynamic_index_in_dim(got, which, 1, keepdims=False)
        return jnp.transpose(part, (1, 0, 2)).reshape(shard + FLAG_ROWS, chips_y * rows)

    cots = jnp.concatenate([cotangents(core), cotangents(1 - core)], axis=1)
    all_rows = jnp.concatenate([own_rows, other_rows], axis=0)
    up_2, all_rows = barrier((up_2, all_rows))
    up_c = jnp.where(offset == 1, mixed_1, up_2)
    weights_all = jnp.concatenate([gate_w, up_w, gate_c, up_c], axis=0)
    proj = project(weights_all, all_rows)
    on_home = cots[shard : shard + 1] > 0.5
    both = jnp.where(on_home, proj[: 2 * shard], proj[2 * shard :])
    gate_val, up_val = both[:shard], both[shard:]
    cotan = cots[:shard].astype(jnp.float32)
    sig_val = jax.nn.sigmoid(gate_val)
    dgate = (cotan * up_val * sig_val * (1.0 + gate_val * (1.0 - sig_val))).astype(jnp.bfloat16)
    dup = (cotan * gate_val * sig_val).astype(jnp.bfloat16)
    terms = jnp.concatenate([dgate, dup], axis=0)
    home_terms = jnp.where(on_home, terms, zero)
    copy_terms = jnp.where(on_home, zero, terms)
    copy_part = jnp.dot(copy_terms, all_rows, preferred_element_type=jnp.float32).astype(jnp.bfloat16)
    copy_g, copy_u = copy_part[:shard], copy_part[shard:]
    first = jnp.where(offset == 1, copy_u, copy_g)
    second = jnp.where(offset == 2, copy_u, zero)
    first, second, copy_g, home_terms, copy_terms = barrier(
        (first, second, copy_g, home_terms, copy_terms)
    )

    ret_1 = lax.ppermute(first, "expert", behind)
    ret_h = lax.ppermute(second, "expert", ring_step(n_exp, 1))
    both_terms = jnp.concatenate([home_terms, copy_terms], axis=0)
    half = chips_y * rows

    def rows_part(terms):
        return lax.dot_general(terms, weights_all, tn, preferred_element_type=jnp.float32)

    dx_oth = rows_part(both_terms[:, half:]).astype(jnp.bfloat16)
    dx_in = lax.ppermute(dx_oth, "dp", swap)
    dx_own, dx_in = barrier((rows_part(both_terms[:, :half]), dx_in))
    dx_pair = (dx_own + dx_in.astype(jnp.float32)).astype(jnp.bfloat16)
    dx_pair, home_terms = barrier((dx_pair, home_terms))
    dx_parts = exchange_y(dx_pair.reshape(chips_y, rows, width))

    home_part = jnp.dot(home_terms, all_rows, preferred_element_type=jnp.float32).astype(jnp.bfloat16)
    ret_1, home_part = barrier((ret_1, home_part))
    sum_g = jnp.where(offset == 1, copy_g, zero).astype(jnp.float32) + jnp.where(offset_next == 2, ret_1, zero).astype(jnp.float32)
    sum_g, home_part = barrier((sum_g.astype(jnp.bfloat16), home_part))
    ret_g = lax.ppermute(sum_g, "expert", behind)
    ret_h, _ = barrier((ret_h, sum_g))
    ret_u = lax.ppermute(ret_h, "expert", onward(n_exp, 1, -2))
    input_grad = jnp.sum(dx_parts.astype(jnp.float32), axis=0).astype(jnp.bfloat16)
    up_part = (
        home_part[shard:].astype(jnp.float32)
        + jnp.where(offset_next == 1, ret_1, zero).astype(jnp.float32)
    ).astype(jnp.bfloat16)
    home_part, up_part, input_grad, ret_g = barrier((home_part, up_part, input_grad, ret_g))
    gate_grad = (home_part[:shard].astype(jnp.float32) + ret_g.astype(jnp.float32)).astype(jnp.bfloat16)
    gate_grad, up_part, ret_u = barrier((gate_grad, up_part, ret_u))
    up_grad = (up_part.astype(jnp.float32) + ret_u.astype(jnp.float32)).astype(jnp.bfloat16)
    return input_grad, gate_grad[None], up_grad[None]


def solution(mesh):
    placed = (
        P(("dp", "expert"), None),
        P(("dp", "expert"), None),
        P("expert", "dp", None),
        P("expert", "dp", None),
        P("expert"),
        P(("dp", "expert")),
        P(("dp", "expert")),
    )
    return jax.shard_map(
        local,
        mesh=mesh,
        in_specs=placed,
        out_specs=(P(("dp", "expert"), None), P("expert", "dp", None), P("expert", "dp", None)),
        check_vma=False,
    )
```
